128 devices in a mesh: row: 8 (over x, y_hi), col: 16 (over z, y_lo, core).
Axes of the slice: x: 4, y: 4 (y_hi: 2, y_lo: 2; y = y_hi * 2 + y_lo), z: 4, core: 2. Of those that a mesh axis runs over, the one named last changes fastest.
Arguments:
- grads: bfloat16 [16384, 4096], P(('row', 'col')), may hold values from -6 to 6
- coeffs: bfloat16 [16384], P(('row', 'col')), may hold values from -4 to 4
- band: int32 [1], replicated, may hold values from 1 to 3
- steps: int32 [128], replicated, may hold values from 0 to 7, as said below
Outputs:
- scores: float32 [16384], P(('row', 'col'))
The draws below stay inside these ranges and needn't reach their ends.
Inputs may be any that keep to these rules, and one draw needn't show every extreme that they name: steps never falls from one block to the next, and every step from 0 to 7 has at least one block.
All inputs are finite; a program needn't handle non-finite values.
Results may differ from the reference program's by a relative error of at most 0.0003.
Values may be sent and summed in bfloat16 or wider, within the bound.
No kernel may reach another device: no remote copies, remote signals or barrier semaphores. Data moves between devices by JAX's collectives and lax.ppermute only.
A program may use at most 64 MiB of HBM per device.

```python
import jax
import jax.numpy as jnp
from jax import lax

F = 4096
EX_DEV = 128
STEPS = 8
NB = 128
N = 16384


def draw_steps(key, part):
    key = jax.random.fold_in(key, 7)
    cuts = jax.random.permutation(key, NB - 1)[:STEPS - 1] + 1
    ids = jnp.arange(NB, dtype=jnp.int32)
    return jnp.sum((ids[:, None] >= cuts[None, :]).astype(jnp.int32), axis=1).astype(jnp.int32)


def block_levels(rng, dims, split, low, top_value):
    loudness = 1.0
    for dim, parts in split:
        heights = jax.random.uniform(jax.random.fold_in(jax.random.fold_in(rng, 6), dim), (parts,), jnp.float32, low / len(split), top_value / len(split))
        loudness = loudness * jnp.repeat(jnp.exp(heights), dims[dim] // parts).reshape((-1,) + (1,) * (len(dims) - 1 - dim))
    return loudness


def centred(rng, extent, deviation, reach, cuts=(), kind=jnp.bfloat16):
    drawn = jax.random.normal(rng, extent, jnp.float32) * deviation
    if len(cuts) > 0:
        drawn = block_levels(rng, extent, cuts, -0.22, 0.18) * drawn
    return jnp.clip(drawn, min=-reach, max=reach).astype(kind)


def setup_inputs(seed: int = 0) -> dict:
    key_of = jax.random.split(jax.random.key(seed), 5)
    grads = centred(key_of[0], (N, F), 1.0, 6.0, ((0, 128),))
    coeffs = centred(key_of[1], (N,), 1.0, 4.0, ((0, 128),))
    band = jax.random.randint(key_of[2], (1,), 1, 4).astype(jnp.int32)
    steps = draw_steps(jax.random.fold_in(key_of[4], 71), 0)
    return {"grads": grads, "coeffs": coeffs, "band": band, "steps": steps}


def reference(grads, coeffs, band, steps):
    width = band[0]
    scale = 1.0 / F ** 0.5
    ex_steps = jnp.repeat(steps, EX_DEV)
    weights = coeffs.astype(jnp.float32)
    blocks = grads.reshape(NB, EX_DEV, F)

    def one_block(inputs):
        rows, srow = inputs
        inner = jnp.dot(rows, grads.T, preferred_element_type=jnp.float32) * scale
        mask = (jnp.abs(ex_steps - srow) <= width).astype(jnp.float32)
        total = lax.optimization_barrier(jnp.sum(jnp.tanh(inner) * (mask * weights)[None, :], axis=1))
        count = EX_DEV * jnp.sum((jnp.abs(steps - srow) <= width).astype(jnp.int32))
        return total / jnp.sqrt(count.astype(jnp.float32))
    return lax.map(one_block, (blocks, steps)).reshape(-1)
```

```python
import functools

import jax
import jax.numpy as jnp
import numpy as np
from jax import lax
from jax.experimental import pallas as pl
from jax.experimental.pallas import tpu as pltpu
from jax.sharding import PartitionSpec as P

AXES = ("row", "col")
SIDE = 4
CHIPS = SIDE**3
LANES = 128

STEPS_OF_PLAN = (
    ((0, 0, 3), (0, 0, 0), True),
    ((3, 0, 0), (0, 0, 0), False),
    ((0, 3, 0), (0, 0, 0), False),
    ((0, 0, 1), (0, 0, 0), True),
    ((1, 0, 0), (0, 0, 0), False),
    ((0, 2, 0), (0, 3, 0), True),
    ((0, 0, 2), (0, 0, 3), True),
    ((2, 0, 0), (3, 0, 0), False),
    ((3, 3, 0), (0, 3, 0), False),
    ((1, 3, 0), (1, 0, 0), False),
    ((0, 2, 3), (0, 2, 0), True),
    ((2, 3, 0), (2, 0, 0), False),
    ((0, 2, 1), (0, 2, 0), True),
    ((0, 2, 2), (0, 2, 3), True),
)


def device_at(x, y, z, core):
    x, y, z, core = x % SIDE, y % SIDE, z % SIDE, core % 2
    return (x * 2 + y // 2) * 16 + z * 4 + (y % 2) * 2 + core


def places():
    for x in range(SIDE):
        for y in range(SIDE):
            for z in range(SIDE):
                for core in range(2):
                    yield x, y, z, core


def on_core(offset, core):
    return tuple(-a for a in offset) if core else tuple(offset)


def shift_pairs(offset):
    pairs = []
    for x, y, z, core in places():
        a, b, c = on_core(offset, core)
        pairs.append((device_at(x + a, y + b, z + c, core), device_at(x, y, z, core)))
    return pairs


def swap_pairs():
    return [(device_at(x, y, z, 1 - c), device_at(x, y, z, c)) for x, y, z, c in places()]


def shift(value, offset):
    return lax.ppermute(value, AXES, shift_pairs(offset))


def minus(a, b):
    return tuple(i - j for i, j in zip(a, b))


def block_table(offsets, other):
    table = np.zeros((2 * CHIPS, len(offsets)), np.int32)
    for x, y, z, core in places():
        fam = 1 - core if other else core
        for k, offset in enumerate(offsets):
            a, b, c = on_core(offset, fam)
            table[device_at(x, y, z, core), k] = device_at(x + a, y + b, z + c, fam)
    return table


def score_kernel(n_rows, n_cols, feats, keep, *refs):
    rows = refs[:n_rows]
    cols = refs[n_rows : n_rows + n_cols]
    out = refs[-1]
    scale = 1.0 / feats**0.5
    right = [r[:, :feats] for r in rows]
    right = right[0] if n_rows == 1 else jnp.concatenate(right, axis=0)
    sums = [jnp.zeros((1, LANES), jnp.float32) for _ in rows]
    for j in range(0, n_cols, 2):
        left = jnp.concatenate([c[:, :feats] for c in cols[j : j + 2]], axis=0)
        inner = lax.dot_general(
            left, right, (((1,), (1,)), ((), ())), preferred_element_type=jnp.float32
        )
        bent = jnp.tanh(inner * scale)
        for h in range(2):
            weights = cols[j + h][:, feats:].astype(jnp.float32)
            for r in range(n_rows):
                part = bent[h * LANES : (h + 1) * LANES, r * LANES : (r + 1) * LANES]
                sums[r] = sums[r] + keep[r, j + h] * jnp.sum(part * weights, axis=0, keepdims=True)
    for r in range(n_rows):
        out[r : r + 1, :] = sums[r]


def row_sums(keep, rows, cols, feats):
    n_rows, n_cols = len(rows), len(cols)

    def body(keep_ref, *refs):
        score_kernel(n_rows, n_cols, feats, keep_ref, *refs)

    tile = 2 * n_rows * n_cols * LANES * LANES
    return pl.pallas_call(
        body,
        out_shape=jax.ShapeDtypeStruct((n_rows, LANES), jnp.float32),
        in_specs=[pl.BlockSpec(memory_space=pltpu.SMEM)]
        + [pl.BlockSpec(memory_space=pltpu.VMEM)] * (n_rows + n_cols),
        out_specs=pl.BlockSpec(memory_space=pltpu.VMEM),
        compiler_params=pltpu.CompilerParams(vmem_limit_bytes=32 * 2**20),
        cost_estimate=pl.CostEstimate(
            flops=tile * feats,
            bytes_accessed=2 * (n_rows + n_cols) * LANES * feats,
            transcendentals=tile // 2,
        ),
    )(keep, *rows, *cols)


def on_device(grads, coeffs, band, steps):
    feats = grads.shape[1]
    rows_here = grads.shape[0]
    width = band[0]
    me = lax.axis_index(AXES)
    zero = (0, 0, 0)
    row_offsets = [zero] + [o for o, _, r in STEPS_OF_PLAN if r]
    col_offsets = [zero] + [o for o, _, r in STEPS_OF_PLAN if not r]

    def steps_at(table):
        mine = lax.dynamic_index_in_dim(jnp.asarray(table), me, 0, keepdims=False)
        hit = mine[:, None] == jnp.arange(steps.shape[0], dtype=jnp.int32)[None, :]
        return jnp.sum(jnp.where(hit, steps[None, :], 0), axis=1)

    row_steps = steps_at(block_table(row_offsets, False))
    col_steps = jnp.concatenate(
        [steps_at(block_table(col_offsets, False)), steps_at(block_table(col_offsets, True))]
    )
    keep = (jnp.abs(row_steps[:, None] - col_steps[None, :]) <= width).astype(jnp.float32)
    count = rows_here * jnp.sum((jnp.abs(steps - row_steps[0]) <= width).astype(jnp.int32))

    held = {
        zero: jnp.concatenate(
            [grads, jnp.broadcast_to(coeffs[:, None], (rows_here, LANES))], axis=1
        )
    }
    for offset, source, _ in STEPS_OF_PLAN:
        held[offset] = shift(held[source], minus(offset, source))
    cols = [held[o] for o in col_offsets]
    cols = cols + [lax.ppermute(c, AXES, swap_pairs()) for c in cols]

    total = None
    for first in range(0, len(row_offsets), 2):
        here = row_offsets[first : first + 2]
        sums = row_sums(keep[first : first + 2], [held[o] for o in here], cols, feats)
        for r, offset in enumerate(here):
            part = sums[r : r + 1]
            if offset != zero:
                part = shift(part, tuple(-a for a in offset))
            total = part if total is None else total + part
    return total.reshape(-1) / jnp.sqrt(count.astype(jnp.float32))


def solution(mesh):
    in_specs = (P(AXES, None), P(AXES), P(), P())
    out_specs = P(AXES)
    return jax.shard_map(
        on_device, mesh=mesh, in_specs=in_specs, out_specs=out_specs, check_vma=False
    )
```

```python
import jax
import jax.numpy as jnp
import numpy as np
from jax import lax
from jax.experimental import pallas as pl
from jax.experimental.pallas import tpu as pltpu
from jax.sharding import PartitionSpec as P

AXES = ("row", "col")
SIDE = 4
LANES = 128
WINDOW = 5

SLOTS = (
    (0, 0, 0), (0, 1, 0), (3, 0, 0), (0, 3, 0), (0, 1, 1), (1, 1, 0), (3, 0, 3),
    (3, 3, 0), (0, 2, 1), (2, 1, 0), (0, 1, 2), (3, 3, 3), (1, 2, 1),
)
PARENT = (None, 0, 0, 0, 1, 1, 2, 2, 4, 5, 4, 7, 8)
OWN = (
    (0, 0, True),
    (6, 0, False), (3, 1, True), (12, 1, False), (3, 2, False), (12, 2, False), (5, 3, False), (6, 3, False),
    (9, 3, True), (10, 3, True), (5, 4, False), (6, 4, False), (9, 4, False), (10, 4, False), (10, 5, False),
    (12, 5, False), (5, 6, False), (10, 6, False), (12, 6, True), (0, 7, False), (4, 7, False), (6, 7, False),
    (12, 7, False), (0, 8, False), (4, 8, False), (6, 8, False), (0, 9, False), (1, 9, True), (0, 10, False),
    (1, 10, True), (9, 10, True), (8, 11, False), (9, 11, False), (8, 12, False), (9, 12, False), (11, 12, False),
)
CROSS = (
    (3, 0, 0), (3, 0, 1), (8, 0, 0), (8, 0, 1), (9, 0, 0), (9, 0, 1), (2, 1, 0), (3, 1, 0), (3, 1, 1), (9, 1, 0),
    (2, 2, 0), (3, 2, 0), (3, 2, 1), (9, 2, 0), (9, 2, 1), (3, 3, 0), (8, 3, 0), (8, 3, 1), (9, 3, 0), (9, 3, 1),
    (3, 4, 0), (3, 4, 1), (8, 4, 0), (8, 4, 1), (9, 4, 0), (9, 4, 1), (1, 5, 0), (4, 5, 0), (4, 5, 1), (6, 5, 0),
    (8, 5, 1), (4, 6, 1), (6, 6, 1), (8, 6, 0), (1, 7, 0), (1, 7, 1), (2, 7, 0), (2, 7, 1), (3, 7, 0), (6, 7, 0),
    (6, 7, 1), (9, 7, 0), (9, 7, 1), (1, 8, 0), (2, 8, 0), (2, 8, 1), (9, 8, 0), (6, 9, 1), (6, 10, 0), (6, 10, 1),
    (3, 11, 0), (3, 11, 1), (4, 11, 1), (6, 11, 0), (6, 11, 1), (9, 11, 0), (9, 11, 1), (3, 12, 0), (3, 12, 1),
    (4, 12, 0), (4, 12, 1), (6, 12, 1), (8, 12, 0), (9, 12, 1),
)
LEAPS = ((0, 0, 0), (3, 0, 0), (3, 0, 3))
HOPS = ((0, 0, 0), (0, 3, 0), (1, 1, 0), (1, 1, 2), (1, 2, 1), (2, 1, 0))
N_SLOTS = len(SLOTS)
PAIRS = ((0,),) + tuple((i, i + 1) for i in range(1, N_SLOTS, 2))
OTHERS = tuple(sorted({j for j, _, _ in CROSS}))


def device_at(x, y, z, core):
    x, y, z, core = x % SIDE, y % SIDE, z % SIDE, core % 2
    return (x * 2 + y // 2) * 16 + z * 4 + (y % 2) * 2 + core


def places():
    for x in range(SIDE):
        for y in range(SIDE):
            for z in range(SIDE):
                for core in range(2):
                    yield x, y, z, core


def on_core(offset, core):
    x, y, z = offset
    return (-x, -z, -y) if core else offset


def plus(a, b):
    return tuple((i + j) % SIDE for i, j in zip(a, b))


def minus(a, b):
    return tuple((i - j) % SIDE for i, j in zip(a, b))


def shift(value, offset):
    pairs = []
    for x, y, z, core in places():
        a, b, c = on_core(offset, core)
        pairs.append((device_at(x + a, y + b, z + c, core), device_at(x, y, z, core)))
    return lax.ppermute(value, AXES, pairs)


def swap(value):
    pairs = [(device_at(x, y, z, 1 - c), device_at(x, y, z, c)) for x, y, z, c in places()]
    return lax.ppermute(value, AXES, pairs)


def held_blocks():
    table = np.zeros((2 * SIDE**3, 2 * N_SLOTS), np.int32)
    for x, y, z, core in places():
        for k, offset in enumerate(SLOTS):
            for other in range(2):
                fam = core ^ other
                a, b, c = on_core(offset, fam)
                at = device_at(x + a, y + b, z + c, fam)
                table[device_at(x, y, z, core), k + other * N_SLOTS] = at
    return table


def pair_weights():
    weights = np.zeros((2, 2, 2 * N_SLOTS, N_SLOTS), np.float32)
    for left, right, one in OWN:
        weights[:, 0, left, right] = 1
        weights[:, 1, left, right] = 0 if one else 1
    for left, right, core in CROSS:
        weights[core, :, N_SLOTS + left, right] = 1
    return weights


def stage_of(slot):
    return next(p for p, pair in enumerate(PAIRS) if slot in pair)


def work_list():
    met = {}
    for left, right, _ in OWN:
        met.setdefault((max(stage_of(left), stage_of(right)), stage_of(right)), set()).add(left)
    for left, right, _ in CROSS:
        key = (max(stage_of(left), stage_of(right)), stage_of(right))
        met.setdefault(key, set()).add(N_SLOTS + left)
    return [
        [(p, sorted(met[(s, p)])) for p in range(len(PAIRS)) if (s, p) in met]
        for s in range(len(PAIRS))
    ]


def add_pairs(work, blocks, sums, weights, feats):
    used = sorted({b for p, lefts in work for b in (*PAIRS[p], *lefts)})
    n_tiles = sum(len(PAIRS[p]) * len(lefts) for p, lefts in work)
    scale = 1.0 / feats**0.5

    def body(w_ref, in_ref, *refs):
        out = refs[-1]
        ref = dict(zip(used, refs))
        out[...] = in_ref[...]
        eye = lax.broadcasted_iota(jnp.int32, (LANES, LANES), 0) == lax.broadcasted_iota(
            jnp.int32, (LANES, LANES), 1
        )

        def coeff(slot):
            return ref[slot][:, feats:].astype(jnp.float32)

        def along(wide):
            return jnp.sum(jnp.where(eye, wide, 0.0), axis=0, keepdims=True)

        for p, lefts in work:
            right = [ref[r][:, :feats] for r in PAIRS[p]]
            right = right[0] if len(right) == 1 else jnp.concatenate(right, axis=0)
            right_coeff = [along(coeff(r)) for r in PAIRS[p]]
            for at in range(0, len(lefts), 2):
                some = lefts[at : at + 2]
                left = [ref[b][:, :feats] for b in some]
                left = left[0] if len(left) == 1 else jnp.concatenate(left, axis=0)
                inner = lax.dot_general(
                    left, right, (((1,), (1,)), ((), ())), preferred_element_type=jnp.float32
                )
                bent = jnp.tanh(inner * scale)
                for h, b in enumerate(some):
                    left_coeff = coeff(b)
                    back = jnp.zeros((LANES, LANES), jnp.float32)
                    for k, r in enumerate(PAIRS[p]):
                        part = bent[h * LANES : (h + 1) * LANES, k * LANES : (k + 1) * LANES]
                        got = jnp.sum(part * left_coeff, axis=0, keepdims=True)
                        out[r : r + 1, :] += w_ref[0, b, r] * got
                        back = back + part * (w_ref[1, b, r] * right_coeff[k])
                    wide = jnp.broadcast_to(jnp.sum(back, axis=1, keepdims=True), (LANES, LANES))
                    out[b : b + 1, :] += along(wide)

    return pl.pallas_call(
        body,
        out_shape=jax.ShapeDtypeStruct(sums.shape, jnp.float32),
        in_specs=[pl.BlockSpec(memory_space=pltpu.SMEM)]
        + [pl.BlockSpec(memory_space=pltpu.VMEM)] * (1 + len(used)),
        out_specs=pl.BlockSpec(memory_space=pltpu.VMEM),
        compiler_params=pltpu.CompilerParams(vmem_limit_bytes=24 * 2**20),
        cost_estimate=pl.CostEstimate(
            flops=2 * n_tiles * LANES * LANES * feats,
            bytes_accessed=2 * len(used) * LANES * feats,
            transcendentals=n_tiles * LANES * LANES,
        ),
    )(weights, sums, *[blocks[b] for b in used])


def on_device(grads, coeffs, band, steps):
    rows_here, feats = grads.shape
    width = band[0]
    me = lax.axis_index(AXES)
    held = lax.dynamic_index_in_dim(jnp.asarray(held_blocks()), me, 0, keepdims=False)
    hit = held[:, None] == jnp.arange(steps.shape[0], dtype=jnp.int32)[None, :]
    held_steps = jnp.sum(jnp.where(hit, steps[None, :], 0), axis=1)
    near = jnp.abs(held_steps[:, None] - held_steps[None, :N_SLOTS]) <= width
    table = pair_weights()
    weights = jnp.where(me % 2 == 0, table[0], table[1])
    weights = jnp.where(near[None], weights, 0.0)
    count = rows_here * jnp.sum((jnp.abs(steps - held_steps[0]) <= width).astype(jnp.int32))

    wide = jnp.broadcast_to(coeffs[:, None], (rows_here, LANES))
    blocks = {0: jnp.concatenate([grads, wide], axis=1)}
    sums = jnp.zeros((2 * N_SLOTS, LANES), jnp.float32)
    after = {}
    work = work_list()

    def held_back(value, *until):
        for u in until:
            value, _ = lax.optimization_barrier((value, u))
        return value

    def fetch(slot, *until):
        offset = minus(SLOTS[slot], SLOTS[PARENT[slot]])
        blocks[slot] = shift(held_back(blocks[PARENT[slot]], *until), offset)

    def turn(slot, *until):
        blocks[N_SLOTS + slot] = swap(held_back(blocks[slot], *until))

    for slot in range(1, N_SLOTS):
        until = [blocks[slot - WINDOW]] if slot > WINDOW else []
        for s, by in GATES:
            if by == slot:
                until.append(after[s])
        fetch(slot, *until)
        for late in SWAPS.get(slot, ()):
            turn(late)
        for s in KERNELS.get(slot, ()):
            sums = add_pairs(work[s], blocks, sums, weights, feats)
            after[s] = sums

    own = sums[:N_SLOTS] + swap(sums[N_SLOTS:])
    ways = {}
    for k, offset in enumerate(SLOTS):
        hop, leap = next(
            (h, l) for l in range(len(LEAPS)) for h in range(len(HOPS))
            if plus(HOPS[h], LEAPS[l]) == offset
        )
        ways.setdefault(leap, {})[hop] = k
    nothing = jnp.zeros((LANES,), jnp.float32)
    there = jnp.zeros((len(HOPS), LANES), jnp.float32)
    for leap, by_hop in ways.items():
        part = jnp.stack([own[by_hop[h]] if h in by_hop else nothing for h in range(len(HOPS))])
        there = there + (shift(part, minus((0, 0, 0), LEAPS[leap])) if leap else part)
    total = there[0:1]
    for h in range(1, len(HOPS)):
        total = total + shift(there[h : h + 1], minus((0, 0, 0), HOPS[h]))
    return total.reshape(-1) / jnp.sqrt(count.astype(jnp.float32))


KERNELS = {6: (0, 1), 9: (2, 3), 11: (4,), 12: (5, 6)}
GATES = ((1, 8), (2, 10), (3, 11), (3, 12))
SWAPS = {5: (2, 3, 1), 8: (4, 6), 10: (8,), 12: (9,)}


def solution(mesh):
    in_specs = (P(AXES, None), P(AXES), P(), P())
    out_specs = P(AXES)
    return jax.shard_map(
        on_device, mesh=mesh, in_specs=in_specs, out_specs=out_specs, check_vma=False
    )
```

```python
import jax
import jax.numpy as jnp
import numpy as np
from jax import lax
from jax.experimental import pallas as pl
from jax.experimental.pallas import tpu as pltpu
from jax.sharding import PartitionSpec as P

AXES = ("row", "col")
SIDE = 4
LANES = 128

SLOTS = (
    (0, 0, 0),
    (0, 1, 0), (3, 0, 0), (0, 3, 0),
    (3, 0, 3), (1, 1, 0), (0, 1, 1),
    (0, 2, 1), (2, 1, 0), (3, 3, 0),
    (3, 3, 3), (1, 2, 1), (0, 1, 2),
)
PARENT = (None, 0, 0, 0, 2, 1, 1, 6, 5, 2, 9, 7, 6)
ROUNDS = ((0,), (1, 2, 3), (4, 5, 6), (7, 8, 9), (10, 11, 12))
OWN = (
    (0, 0, True), (1, 0, False), (6, 0, False), (11, 0, False), (12, 0, False), (5, 1, False), (8, 1, True),
    (11, 1, False), (12, 1, True), (5, 2, False), (8, 2, False), (11, 2, False), (12, 2, False), (1, 3, True),
    (6, 3, False), (11, 3, False), (12, 3, True), (0, 4, False), (7, 4, False), (11, 4, True), (12, 4, False),
    (0, 5, False), (4, 5, False), (7, 5, False), (12, 5, False), (5, 6, False), (8, 6, False), (10, 7, False),
    (12, 7, False), (10, 8, False), (12, 8, True), (5, 9, True), (8, 9, False), (9, 10, False), (9, 11, False),
    (10, 11, False),
)
CROSS = (
    (3, 0, 0), (3, 0, 1), (8, 0, 0), (8, 0, 1), (9, 0, 0), (9, 0, 1), (2, 1, 0), (2, 1, 1), (5, 1, 1),
    (9, 1, 0), (9, 1, 1), (2, 2, 1), (5, 2, 0), (5, 2, 1), (9, 2, 0), (9, 2, 1), (3, 3, 1), (8, 3, 0),
    (8, 3, 1), (9, 3, 1), (5, 4, 1), (8, 4, 0), (9, 4, 0), (9, 4, 1), (5, 5, 1), (6, 5, 0), (6, 5, 1),
    (7, 5, 1), (8, 5, 1), (9, 5, 0), (9, 5, 1), (6, 6, 0), (7, 6, 0), (7, 6, 1), (8, 6, 0), (8, 6, 1),
    (2, 7, 0), (2, 7, 1), (8, 7, 1), (2, 8, 0), (2, 8, 1), (8, 8, 0), (7, 9, 0), (7, 9, 1), (8, 9, 0),
    (8, 9, 1), (2, 10, 0), (3, 10, 0), (3, 10, 1), (6, 10, 0), (8, 10, 0), (8, 10, 1), (9, 10, 0), (9, 10, 1),
    (2, 11, 0), (2, 11, 1), (3, 11, 0), (3, 11, 1), (6, 11, 0), (6, 11, 1), (7, 11, 0), (8, 11, 0), (9, 11, 0),
    (9, 11, 1),
)
LEAPS = ((0, 0, 0), (0, 2, 0), (0, 1, 1), (2, 2, 0), (3, 0, 3))
HOPS = ((0, 0, 0), (0, 0, 1), (0, 3, 0), (1, 1, 0))
N_SLOTS = len(SLOTS)
PAIRS = ((0, 3), (1, 2), (4, 5), (6, 9), (7, 8), (10, 11), (12,))
OTHERS = tuple(sorted({j for j, _, _ in CROSS}))


def device_at(x, y, z, core):
    x, y, z, core = x % SIDE, y % SIDE, z % SIDE, core % 2
    return (x * 2 + y // 2) * 16 + z * 4 + (y % 2) * 2 + core


def places():
    for x in range(SIDE):
        for y in range(SIDE):
            for z in range(SIDE):
                for core in range(2):
                    yield x, y, z, core


def on_core(offset, core):
    x, y, z = offset
    return (-x, -z, -y) if core else offset


def plus(a, b):
    return tuple((i + j) % SIDE for i, j in zip(a, b))


def minus(a, b):
    return tuple((i - j) % SIDE for i, j in zip(a, b))


def shift(value, offset):
    pairs = []
    for x, y, z, core in places():
        a, b, c = on_core(offset, core)
        pairs.append((device_at(x + a, y + b, z + c, core), device_at(x, y, z, core)))
    return lax.ppermute(value, AXES, pairs)


def swap(value):
    pairs = [(device_at(x, y, z, 1 - c), device_at(x, y, z, c)) for x, y, z, c in places()]
    return lax.ppermute(value, AXES, pairs)


def held_blocks():
    table = np.zeros((2 * SIDE**3, 2 * N_SLOTS), np.int32)
    for x, y, z, core in places():
        for k, offset in enumerate(SLOTS):
            for other in range(2):
                fam = core ^ other
                a, b, c = on_core(offset, fam)
                at = device_at(x + a, y + b, z + c, fam)
                table[device_at(x, y, z, core), k + other * N_SLOTS] = at
    return table


def pair_weights():
    weights = np.zeros((2, 2, 2 * N_SLOTS, N_SLOTS), np.float32)
    for left, right, one in OWN:
        weights[:, 0, left, right] = 1
        weights[:, 1, left, right] = 0 if one else 1
    for left, right, core in CROSS:
        weights[core, :, N_SLOTS + left, right] = 1
    return weights


def work_list():
    came = {slot: n for n, slots in enumerate(ROUNDS) for slot in slots}
    met = {}
    for left, right, _ in OWN:
        met.setdefault((max(came[left], came[right]), right), set()).add(left)
    for left, right, _ in CROSS:
        met.setdefault((max(came[left], came[right]), right), set()).add(N_SLOTS + left)
    work = []
    for n in range(len(ROUNDS)):
        here = []
        for pair in PAIRS:
            lefts = set().union(*(met.get((n, r), set()) for r in pair))
            rights = tuple(r for r in pair if came[r] <= n)
            if lefts:
                counted = {b: [r for r in rights if b in met.get((n, r), ())] for b in lefts}
                here.append((rights, sorted(lefts), counted))
        work.append(here)
    return work


def add_pairs(work, blocks, sums, weights, feats):
    used = sorted({b for rights, lefts, _ in work for b in (*rights, *lefts)})
    n_tiles = sum(len(rights) * len(lefts) for rights, lefts, _ in work)
    scale = 1.0 / feats**0.5

    def body(w_ref, in_ref, *refs):
        out = refs[-1]
        ref = dict(zip(used, refs))
        out[...] = in_ref[...]
        eye = lax.broadcasted_iota(jnp.int32, (LANES, LANES), 0) == lax.broadcasted_iota(
            jnp.int32, (LANES, LANES), 1
        )

        def coeff(slot):
            return ref[slot][:, feats:].astype(jnp.float32)

        def along(wide):
            return jnp.sum(jnp.where(eye, wide, 0.0), axis=0, keepdims=True)

        def down(wide):
            return jnp.sum(jnp.where(eye, wide, 0.0), axis=1, keepdims=True)

        for rights, lefts, counted in work:
            right = [ref[r][:, :feats] for r in rights]
            right = right[0] if len(right) == 1 else jnp.concatenate(right, axis=0)
            right_coeff = [coeff(r)[0:1, :] for r in rights]
            for at in range(0, len(lefts), 2):
                some = lefts[at : at + 2]
                left = [ref[b][:, :feats] for b in some]
                left = left[0] if len(left) == 1 else jnp.concatenate(left, axis=0)
                inner = lax.dot_general(
                    left, right, (((1,), (1,)), ((), ())), preferred_element_type=jnp.float32
                )
                bent = jnp.tanh(inner * scale)
                for h, b in enumerate(some):
                    left_coeff = down(coeff(b))
                    back = jnp.zeros((LANES, LANES), jnp.float32)
                    for k, r in enumerate(rights):
                        if r not in counted[b]:
                            continue
                        part = bent[h * LANES : (h + 1) * LANES, k * LANES : (k + 1) * LANES]
                        got = jnp.sum(part * left_coeff, axis=0, keepdims=True)
                        out[r : r + 1, :] += w_ref[0, b, r] * got
                        back = back + part * (w_ref[1, b, r] * right_coeff[k])
                    wide = jnp.broadcast_to(jnp.sum(back, axis=1, keepdims=True), (LANES, LANES))
                    out[b : b + 1, :] += along(wide)

    return pl.pallas_call(
        body,
        out_shape=jax.ShapeDtypeStruct(sums.shape, jnp.float32),
        in_specs=[pl.BlockSpec(memory_space=pltpu.SMEM)]
        + [pl.BlockSpec(memory_space=pltpu.VMEM)] * (1 + len(used)),
        out_specs=pl.BlockSpec(memory_space=pltpu.VMEM),
        compiler_params=pltpu.CompilerParams(vmem_limit_bytes=24 * 2**20),
        cost_estimate=pl.CostEstimate(
            flops=2 * n_tiles * LANES * LANES * feats,
            bytes_accessed=2 * len(used) * LANES * feats,
            transcendentals=n_tiles * LANES * LANES,
        ),
    )(weights, sums, *[blocks[b] for b in used])


def on_device(grads, coeffs, band, steps):
    rows_here, feats = grads.shape
    width = band[0]
    me = lax.axis_index(AXES)
    held = lax.dynamic_index_in_dim(jnp.asarray(held_blocks()), me, 0, keepdims=False)
    hit = held[:, None] == jnp.arange(steps.shape[0], dtype=jnp.int32)[None, :]
    held_steps = jnp.sum(jnp.where(hit, steps[None, :], 0), axis=1)
    near = jnp.abs(held_steps[:, None] - held_steps[None, :N_SLOTS]) <= width
    table = pair_weights()
    weights = jnp.where(me % 2 == 0, table[0], table[1])
    weights = jnp.where(near[None], weights, 0.0)
    count = rows_here * jnp.sum((jnp.abs(steps - held_steps[0]) <= width).astype(jnp.int32))

    divisor = jnp.sqrt(count.astype(jnp.float32))
    weights, divisor = lax.optimization_barrier((weights, divisor))
    wide = jnp.broadcast_to(coeffs[None, :], (LANES, rows_here))
    blocks = {0: jnp.concatenate([grads, wide], axis=1)}
    sums = jnp.zeros((2 * N_SLOTS, LANES), jnp.float32)
    work = work_list()

    def held_back(value, until):
        for u in until:
            value, _ = lax.optimization_barrier((value, u))
        return value

    for n in range(1, len(ROUNDS)):
        until = [blocks[slot] for slot in ROUNDS[n - 1]] if n > 1 else []
        for at, slot in enumerate(ROUNDS[n]):
            parent = PARENT[slot]
            blocks[slot] = shift(
                held_back(blocks[parent], until[at : at + 1]), minus(SLOTS[slot], SLOTS[parent])
            )
        if n == len(ROUNDS) - 1:
            sums = add_pairs(work[0], blocks, held_back(sums, until), weights, feats)
            until = until + [sums]
        for slot in ROUNDS[n - 1] if n > 1 else ():
            if slot in OTHERS:
                blocks[N_SLOTS + slot] = swap(held_back(blocks[slot], until))
    sums = add_pairs(sum(work[1:-1], []), blocks, sums, weights, feats)
    sums = add_pairs(work[-1], blocks, sums, weights, feats)

    own = sums[:N_SLOTS] + swap(sums[N_SLOTS:])
    ways = {}
    for k, offset in enumerate(SLOTS):
        hop, leap = next(
            (h, l) for l in range(len(LEAPS)) for h in range(len(HOPS))
            if plus(HOPS[h], LEAPS[l]) == offset
        )
        ways.setdefault(leap, {})[hop] = k
    nothing = jnp.zeros((LANES,), jnp.float32)
    there = jnp.zeros((len(HOPS), LANES), jnp.float32)
    for leap, by_hop in ways.items():
        part = jnp.stack([own[by_hop[h]] if h in by_hop else nothing for h in range(len(HOPS))])
        there = there + (shift(part, minus((0, 0, 0), LEAPS[leap])) if leap else part)
    total = there[0:1]
    for h in range(1, len(HOPS)):
        total = total + shift(there[h : h + 1], minus((0, 0, 0), HOPS[h]))
    return total.reshape(-1) / divisor


def solution(mesh):
    in_specs = (P(AXES, None), P(AXES), P(), P())
    out_specs = P(AXES)
    return jax.shard_map(
        on_device, mesh=mesh, in_specs=in_specs, out_specs=out_specs, check_vma=False
    )
```

```python
import jax
import jax.numpy as jnp
import numpy as np
from jax import lax
from jax.experimental import pallas as pl
from jax.experimental.pallas import tpu as pltpu
from jax.sharding import PartitionSpec as P

AXES = ("row", "col")
SIDE = 4
LANES = 128

SLOTS = (
    (0, 0, 0),
    (0, 1, 0), (3, 0, 0), (0, 3, 0),
    (3, 0, 3), (1, 1, 0), (0, 1, 1),
    (0, 2, 1), (2, 1, 0), (3, 3, 0),
    (3, 3, 3), (1, 2, 1), (0, 1, 2),
)
PARENT = (None, 0, 0, 0, 2, 1, 1, 6, 5, 2, 9, 7, 6)
ROUNDS = ((0,), (1, 2, 3), (4, 5, 6), (7, 8, 9), (10, 11, 12))
OWN = (
    (0, 0, True), (1, 0, False), (6, 0, False), (11, 0, False), (12, 0, False), (5, 1, False), (8, 1, True),
    (11, 1, False), (12, 1, True), (5, 2, False), (8, 2, False), (11, 2, False), (12, 2, False), (1, 3, True),
    (6, 3, False), (11, 3, False), (12, 3, True), (0, 4, False), (7, 4, False), (11, 4, True), (12, 4, False),
    (0, 5, False), (4, 5, False), (7, 5, False), (12, 5, False), (5, 6, False), (8, 6, False), (10, 7, False),
    (12, 7, False), (10, 8, False), (12, 8, True), (5, 9, True), (8, 9, False), (9, 10, False), (9, 11, False),
    (10, 11, False),
)
CROSS = (
    (3, 0, 0), (3, 0, 1), (8, 0, 0), (8, 0, 1), (9, 0, 0), (9, 0, 1), (2, 1, 0), (2, 1, 1), (5, 1, 1),
    (9, 1, 0), (9, 1, 1), (2, 2, 1), (5, 2, 0), (5, 2, 1), (9, 2, 0), (9, 2, 1), (3, 3, 1), (8, 3, 0),
    (8, 3, 1), (9, 3, 1), (5, 4, 1), (8, 4, 0), (9, 4, 0), (9, 4, 1), (5, 5, 1), (6, 5, 0), (6, 5, 1),
    (7, 5, 1), (8, 5, 1), (9, 5, 0), (9, 5, 1), (6, 6, 0), (7, 6, 0), (7, 6, 1), (8, 6, 0), (8, 6, 1),
    (2, 7, 0), (2, 7, 1), (8, 7, 1), (2, 8, 0), (2, 8, 1), (8, 8, 0), (7, 9, 0), (7, 9, 1), (8, 9, 0),
    (8, 9, 1), (2, 10, 0), (3, 10, 0), (3, 10, 1), (6, 10, 0), (8, 10, 0), (8, 10, 1), (9, 10, 0), (9, 10, 1),
    (2, 11, 0), (2, 11, 1), (3, 11, 0), (3, 11, 1), (6, 11, 0), (6, 11, 1), (7, 11, 0), (8, 11, 0), (9, 11, 0),
    (9, 11, 1),
)
N_SLOTS = len(SLOTS)
PAIRS = ((0, 3), (1, 2), (4, 5), (6, 9), (7, 8), (10, 11), (12,))
OTHERS = tuple(sorted({j for j, _, _ in CROSS}))


def device_at(x, y, z, core):
    x, y, z, core = x % SIDE, y % SIDE, z % SIDE, core % 2
    return (x * 2 + y // 2) * 16 + z * 4 + (y % 2) * 2 + core


def places():
    for x in range(SIDE):
        for y in range(SIDE):
            for z in range(SIDE):
                for core in range(2):
                    yield x, y, z, core


def on_core(offset, core):
    x, y, z = offset
    return (-x, -z, -y) if core else offset


def plus(a, b):
    return tuple((i + j) % SIDE for i, j in zip(a, b))


def minus(a, b):
    return tuple((i - j) % SIDE for i, j in zip(a, b))


def shift(value, offset):
    pairs = []
    for x, y, z, core in places():
        a, b, c = on_core(offset, core)
        pairs.append((device_at(x + a, y + b, z + c, core), device_at(x, y, z, core)))
    return lax.ppermute(value, AXES, pairs)


def swap(value):
    pairs = [(device_at(x, y, z, 1 - c), device_at(x, y, z, c)) for x, y, z, c in places()]
    return lax.ppermute(value, AXES, pairs)


def held_blocks():
    table = np.zeros((2 * SIDE**3, 2 * N_SLOTS), np.int32)
    for x, y, z, core in places():
        for k, offset in enumerate(SLOTS):
            for other in range(2):
                fam = core ^ other
                a, b, c = on_core(offset, fam)
                at = device_at(x + a, y + b, z + c, fam)
                table[device_at(x, y, z, core), k + other * N_SLOTS] = at
    return table


def pair_weights():
    weights = np.zeros((2, 2, 2 * N_SLOTS, N_SLOTS), np.float32)
    for left, right, one in OWN:
        weights[:, 0, left, right] = 1
        weights[:, 1, left, right] = 0 if one else 1
    for left, right, core in CROSS:
        weights[core, :, N_SLOTS + left, right] = 1
    return weights


def work_list():
    came = {slot: n for n, slots in enumerate(ROUNDS) for slot in slots}
    met = {}
    for left, right, _ in OWN:
        met.setdefault((max(came[left], came[right]), right), set()).add(left)
    for left, right, _ in CROSS:
        met.setdefault((max(came[left], came[right]), right), set()).add(N_SLOTS + left)
    work = []
    for n in range(len(ROUNDS)):
        here = []
        for pair in PAIRS:
            lefts = set().union(*(met.get((n, r), set()) for r in pair))
            rights = tuple(r for r in pair if came[r] <= n)
            if lefts:
                counted = {b: [r for r in rights if b in met.get((n, r), ())] for b in lefts}
                here.append((rights, sorted(lefts), counted))
        work.append(here)
    return work


def add_pairs(work, blocks, sums, weights, feats):
    used = sorted({b for rights, lefts, _ in work for b in (*rights, *lefts)})
    n_tiles = sum(len(rights) * len(lefts) for rights, lefts, _ in work)
    scale = 1.0 / feats**0.5

    def body(w_ref, in_ref, *refs):
        out = refs[-1]
        ref = dict(zip(used, refs))
        out[...] = in_ref[...]
        eye = lax.broadcasted_iota(jnp.int32, (LANES, LANES), 0) == lax.broadcasted_iota(
            jnp.int32, (LANES, LANES), 1
        )

        def coeff(slot):
            return ref[slot][:, feats:].astype(jnp.float32)

        def along(wide):
            return jnp.sum(jnp.where(eye, wide, 0.0), axis=0, keepdims=True)

        def down(wide):
            return jnp.sum(jnp.where(eye, wide, 0.0), axis=1, keepdims=True)

        for rights, lefts, counted in work:
            right = [ref[r][:, :feats] for r in rights]
            right = right[0] if len(right) == 1 else jnp.concatenate(right, axis=0)
            right_coeff = [coeff(r)[0:1, :] for r in rights]
            for at in range(0, len(lefts), 2):
                some = lefts[at : at + 2]
                left = [ref[b][:, :feats] for b in some]
                left = left[0] if len(left) == 1 else jnp.concatenate(left, axis=0)
                inner = lax.dot_general(
                    left, right, (((1,), (1,)), ((), ())), preferred_element_type=jnp.float32
                )
                bent = jnp.tanh(inner * scale)
                for h, b in enumerate(some):
                    left_coeff = down(coeff(b))
                    back = jnp.zeros((LANES, LANES), jnp.float32)
                    for k, r in enumerate(rights):
                        if r not in counted[b]:
                            continue
                        part = bent[h * LANES : (h + 1) * LANES, k * LANES : (k + 1) * LANES]
                        got = jnp.sum(part * left_coeff, axis=0, keepdims=True)
                        out[r : r + 1, :] += w_ref[0, b, r] * got
                        back = back + part * (w_ref[1, b, r] * right_coeff[k])
                    wide = jnp.broadcast_to(jnp.sum(back, axis=1, keepdims=True), (LANES, LANES))
                    out[b : b + 1, :] += along(wide)

    return pl.pallas_call(
        body,
        out_shape=jax.ShapeDtypeStruct(sums.shape, jnp.float32),
        in_specs=[pl.BlockSpec(memory_space=pltpu.SMEM)]
        + [pl.BlockSpec(memory_space=pltpu.VMEM)] * (1 + len(used)),
        out_specs=pl.BlockSpec(memory_space=pltpu.VMEM),
        compiler_params=pltpu.CompilerParams(vmem_limit_bytes=24 * 2**20),
        cost_estimate=pl.CostEstimate(
            flops=2 * n_tiles * LANES * LANES * feats,
            bytes_accessed=2 * len(used) * LANES * feats,
            transcendentals=n_tiles * LANES * LANES,
        ),
    )(weights, sums, *[blocks[b] for b in used])


def on_device(grads, coeffs, band, steps):
    rows_here, feats = grads.shape
    width = band[0]
    me = lax.axis_index(AXES)
    held = lax.dynamic_index_in_dim(jnp.asarray(held_blocks()), me, 0, keepdims=False)
    hit = held[:, None] == jnp.arange(steps.shape[0], dtype=jnp.int32)[None, :]
    held_steps = jnp.sum(jnp.where(hit, steps[None, :], 0), axis=1)
    near = jnp.abs(held_steps[:, None] - held_steps[None, :N_SLOTS]) <= width
    table = pair_weights()
    weights = jnp.where(me % 2 == 0, table[0], table[1])
    weights = jnp.where(near[None], weights, 0.0)
    count = rows_here * jnp.sum((jnp.abs(steps - held_steps[0]) <= width).astype(jnp.int32))

    divisor = jnp.sqrt(count.astype(jnp.float32))
    weights, divisor = lax.optimization_barrier((weights, divisor))
    wide = jnp.broadcast_to(coeffs[None, :], (LANES, rows_here))
    blocks = {0: jnp.concatenate([grads, wide], axis=1)}
    sums = jnp.zeros((2 * N_SLOTS, LANES), jnp.float32)
    work = work_list()

    def held_back(value, until):
        for u in until:
            value, _ = lax.optimization_barrier((value, u))
        return value

    for n in range(1, len(ROUNDS)):
        until = [blocks[slot] for slot in ROUNDS[n - 1]] if n > 1 else []
        for at, slot in enumerate(ROUNDS[n]):
            parent = PARENT[slot]
            blocks[slot] = shift(
                held_back(blocks[parent], until[at : at + 1]), minus(SLOTS[slot], SLOTS[parent])
            )
        if n == len(ROUNDS) - 1:
            sums = add_pairs(work[0], blocks, held_back(sums, until), weights, feats)
            until = until + [sums]
        for slot in ROUNDS[n - 1] if n > 1 else ():
            if slot in OTHERS:
                blocks[N_SLOTS + slot] = swap(held_back(blocks[slot], until))
    sums = add_pairs(sum(work[1:-1], []), blocks, sums, weights, feats)
    sums = add_pairs(work[-1], blocks, sums, weights, feats)

    home = held[None, :] == jnp.arange(2 * SIDE**3, dtype=jnp.int32)[:, None]
    parts = jnp.sum(jnp.where(home[:, :, None], sums[None], 0.0), axis=1)
    total = jnp.sum(lax.all_to_all(parts, AXES, 0, 0, tiled=True), axis=0)
    return total.reshape(-1) / divisor


def solution(mesh):
    in_specs = (P(AXES, None), P(AXES), P(), P())
    out_specs = P(AXES)
    return jax.shard_map(
        on_device, mesh=mesh, in_specs=in_specs, out_specs=out_specs, check_vma=False
    )
```

```python
import jax
import jax.numpy as jnp
import numpy as np
from jax import lax
from jax.experimental import pallas as pl
from jax.experimental.pallas import tpu as pltpu
from jax.sharding import PartitionSpec as P

AXES = ("row", "col")
SIDE = 4
LANES = 128

SLOTS = (
    (0, 0, 0),
    (3, 0, 0), (0, 1, 0), (0, 3, 0),
    (1, 1, 0), (3, 0, 1), (0, 3, 3),
    (3, 3, 3), (3, 1, 1), (3, 0, 2),
    (2, 3, 3), (1, 2, 0), (3, 1, 2),
)
PARENT = (None, 0, 0, 0, 2, 1, 3, 6, 5, 5, 7, 4, 8)
ROUNDS = ((0,), (1, 2, 3), (4, 6, 5), (7, 8, 9), (10, 11, 12))
OWN = (
    (0, 0, True), (9, 0, False), (3, 1, False), (4, 1, False), (6, 1, False), (7, 1, False), (9, 1, True),
    (3, 2, True), (4, 2, False), (6, 2, False), (7, 2, False), (9, 2, False), (9, 3, False), (0, 4, False),
    (5, 4, False), (9, 4, False), (0, 5, False), (9, 5, False), (8, 6, False), (10, 6, True), (11, 6, False),
    (3, 7, False), (4, 7, False), (5, 7, False), (8, 7, True), (3, 8, False), (4, 8, False), (5, 8, False),
    (8, 9, False), (10, 9, False), (11, 9, True), (0, 10, False), (1, 10, False), (0, 11, False), (1, 11, True),
    (4, 12, True),
)
CROSS = (
    (0, 0, 1), (4, 0, 0), (4, 0, 1), (6, 0, 0), (2, 1, 0), (2, 1, 1), (8, 1, 0), (9, 1, 0), (9, 1, 1),
    (2, 2, 0), (8, 2, 0), (8, 2, 1), (4, 3, 1), (6, 3, 0), (6, 3, 1), (7, 3, 0), (7, 3, 1), (1, 4, 0),
    (1, 4, 1), (2, 4, 1), (3, 4, 1), (6, 4, 0), (6, 4, 1), (8, 4, 0), (8, 4, 1), (1, 5, 0), (1, 5, 1),
    (2, 5, 0), (2, 5, 1), (3, 5, 1), (6, 5, 0), (6, 5, 1), (8, 5, 0), (8, 5, 1), (2, 6, 0), (2, 6, 1),
    (6, 6, 0), (7, 6, 1), (0, 7, 1), (8, 7, 1), (0, 8, 1), (8, 8, 1), (7, 9, 0), (7, 9, 1), (0, 10, 0),
    (1, 10, 1), (2, 10, 0), (2, 10, 1), (3, 10, 0), (3, 10, 1), (7, 10, 0), (8, 10, 0), (0, 11, 0), (0, 11, 1),
    (1, 11, 0), (1, 11, 1), (2, 11, 0), (2, 11, 1), (3, 11, 0), (3, 11, 1), (8, 11, 0), (8, 11, 1), (2, 12, 0),
    (2, 12, 1),
)
N_SLOTS = len(SLOTS)
PAIRS = ((0, 3), (1, 2), (4, 5), (6, 9), (7, 8), (10, 11), (12,))
OTHERS = tuple(sorted({j for j, _, _ in CROSS}))


def device_at(x, y, z, core):
    x, y, z, core = x % SIDE, y % SIDE, z % SIDE, core % 2
    return (x * 2 + y // 2) * 16 + z * 4 + (y % 2) * 2 + core


def places():
    for x in range(SIDE):
        for y in range(SIDE):
            for z in range(SIDE):
                for core in range(2):
                    yield x, y, z, core


def on_core(offset, core):
    x, y, z = offset
    return (-x, -z, -y) if core else offset


def minus(a, b):
    return tuple((i - j) % SIDE for i, j in zip(a, b))


def shift(value, offset):
    pairs = []
    for x, y, z, core in places():
        a, b, c = on_core(offset, core)
        pairs.append((device_at(x + a, y + b, z + c, core), device_at(x, y, z, core)))
    return lax.ppermute(value, AXES, pairs)


def swap(value):
    pairs = [(device_at(x, y, z, 1 - c), device_at(x, y, z, c)) for x, y, z, c in places()]
    return lax.ppermute(value, AXES, pairs)


def held_blocks():
    table = np.zeros((2 * SIDE**3, 2 * N_SLOTS), np.int32)
    for x, y, z, core in places():
        for k, offset in enumerate(SLOTS):
            for other in range(2):
                fam = core ^ other
                a, b, c = on_core(offset, fam)
                at = device_at(x + a, y + b, z + c, fam)
                table[device_at(x, y, z, core), k + other * N_SLOTS] = at
    return table


def pair_weights():
    weights = np.zeros((2, 2, 2 * N_SLOTS, N_SLOTS), np.float32)
    for left, right, one in OWN:
        weights[:, 0, left, right] = 1
        weights[:, 1, left, right] = 0 if one else 1
    for left, right, core in CROSS:
        weights[core, :, N_SLOTS + left, right] = 1
    return weights


def work_list():
    came = {slot: n for n, slots in enumerate(ROUNDS) for slot in slots}
    met = {}
    for left, right, _ in OWN:
        met.setdefault((max(came[left], came[right]), right), set()).add(left)
    for left, right, _ in CROSS:
        met.setdefault((max(came[left], came[right]), right), set()).add(N_SLOTS + left)
    work = []
    for n in range(len(ROUNDS)):
        here = []
        for pair in PAIRS:
            lefts = set().union(*(met.get((n, r), set()) for r in pair))
            rights = tuple(r for r in pair if came[r] <= n)
            if lefts:
                counted = {b: [r for r in rights if b in met.get((n, r), ())] for b in lefts}
                here.append((rights, sorted(lefts), counted))
        work.append(here)
    return work


def add_pairs(work, blocks, sums, weights, feats):
    used = sorted({b for rights, lefts, _ in work for b in (*rights, *lefts)})
    n_tiles = sum(len(rights) * len(lefts) for rights, lefts, _ in work)
    scale = 1.0 / feats**0.5

    def body(w_ref, in_ref, *refs):
        out = refs[-1]
        ref = dict(zip(used, refs))
        out[...] = in_ref[...]
        eye = lax.broadcasted_iota(jnp.int32, (LANES, LANES), 0) == lax.broadcasted_iota(
            jnp.int32, (LANES, LANES), 1
        )

        def coeff(slot):
            return ref[slot][:, feats:].astype(jnp.float32)

        def along(wide):
            return jnp.sum(jnp.where(eye, wide, 0.0), axis=0, keepdims=True)

        def down(wide):
            return jnp.sum(jnp.where(eye, wide, 0.0), axis=1, keepdims=True)

        for rights, lefts, counted in work:
            right = [ref[r][:, :feats] for r in rights]
            right = right[0] if len(right) == 1 else jnp.concatenate(right, axis=0)
            right_coeff = [coeff(r)[0:1, :] for r in rights]
            for at in range(0, len(lefts), 2):
                some = lefts[at : at + 2]
                left = [ref[b][:, :feats] for b in some]
                left = left[0] if len(left) == 1 else jnp.concatenate(left, axis=0)
                inner = lax.dot_general(
                    left, right, (((1,), (1,)), ((), ())), preferred_element_type=jnp.float32
                )
                bent = jnp.tanh(inner * scale)
                for h, b in enumerate(some):
                    left_coeff = down(coeff(b))
                    back = jnp.zeros((LANES, LANES), jnp.float32)
                    for k, r in enumerate(rights):
                        if r not in counted[b]:
                            continue
                        part = bent[h * LANES : (h + 1) * LANES, k * LANES : (k + 1) * LANES]
                        got = jnp.sum(part * left_coeff, axis=0, keepdims=True)
                        out[r : r + 1, :] += w_ref[0, b, r] * got
                        back = back + part * (w_ref[1, b, r] * right_coeff[k])
                    wide = jnp.broadcast_to(jnp.sum(back, axis=1, keepdims=True), (LANES, LANES))
                    out[b : b + 1, :] += along(wide)

    return pl.pallas_call(
        body,
        out_shape=jax.ShapeDtypeStruct(sums.shape, jnp.float32),
        in_specs=[pl.BlockSpec(memory_space=pltpu.SMEM)]
        + [pl.BlockSpec(memory_space=pltpu.VMEM)] * (1 + len(used)),
        out_specs=pl.BlockSpec(memory_space=pltpu.VMEM),
        compiler_params=pltpu.CompilerParams(vmem_limit_bytes=24 * 2**20),
        cost_estimate=pl.CostEstimate(
            flops=2 * n_tiles * LANES * LANES * feats,
            bytes_accessed=2 * len(used) * LANES * feats,
            transcendentals=n_tiles * LANES * LANES,
        ),
    )(weights, sums, *[blocks[b] for b in used])


def on_device(grads, coeffs, band, steps):
    rows_here, feats = grads.shape
    width = band[0]
    me = lax.axis_index(AXES)
    held = lax.dynamic_index_in_dim(jnp.asarray(held_blocks()), me, 0, keepdims=False)
    hit = held[:, None] == jnp.arange(steps.shape[0], dtype=jnp.int32)[None, :]
    held_steps = jnp.sum(jnp.where(hit, steps[None, :], 0), axis=1)
    near = jnp.abs(held_steps[:, None] - held_steps[None, :N_SLOTS]) <= width
    table = pair_weights()
    weights = jnp.where(me % 2 == 0, table[0], table[1])
    weights = jnp.where(near[None], weights, 0.0)
    count = rows_here * jnp.sum((jnp.abs(steps - held_steps[0]) <= width).astype(jnp.int32))

    divisor = jnp.sqrt(count.astype(jnp.float32))
    weights, divisor = lax.optimization_barrier((weights, divisor))
    wide = jnp.broadcast_to(coeffs[None, :], (LANES, rows_here))
    blocks = {0: jnp.concatenate([grads, wide], axis=1)}
    sums = jnp.zeros((2 * N_SLOTS, LANES), jnp.float32)
    work = work_list()

    def held_back(value, until):
        for u in until:
            value, _ = lax.optimization_barrier((value, u))
        return value

    if 0 in OTHERS:
        blocks[N_SLOTS] = swap(blocks[0])
    for n in range(1, len(ROUNDS)):
        until = [blocks[slot] for slot in ROUNDS[n - 1]] if n > 1 else []
        for at, slot in enumerate(ROUNDS[n]):
            parent = PARENT[slot]
            blocks[slot] = shift(
                held_back(blocks[parent], until[at : at + 1]), minus(SLOTS[slot], SLOTS[parent])
            )
        if n == 3:
            sums = add_pairs(work[0] + work[1], blocks, sums, weights, feats)
            until = until[:2] + [sums]
        if n == 4:
            sums = jnp.where(width < 0, 0.0, held_back(sums, until))
            until = until + [sums]
        for slot in ROUNDS[n - 1] if n > 1 else ():
            if slot in OTHERS:
                blocks[N_SLOTS + slot] = swap(held_back(blocks[slot], until))
    sums = add_pairs(work[2] + work[3], blocks, sums, weights, feats)
    sums = add_pairs(work[4], blocks, sums, weights, feats)

    home = held[None, :] == jnp.arange(2 * SIDE**3, dtype=jnp.int32)[:, None]
    parts = jnp.sum(jnp.where(home[:, :, None], sums[None], 0.0), axis=1)
    total = jnp.sum(lax.all_to_all(parts, AXES, 0, 0, tiled=True), axis=0)
    return total.reshape(-1) / divisor


def solution(mesh):
    in_specs = (P(AXES, None), P(AXES), P(), P())
    out_specs = P(AXES)
    return jax.shard_map(
        on_device, mesh=mesh, in_specs=in_specs, out_specs=out_specs, check_vma=False
    )
```

```python
import jax
import jax.numpy as jnp
import numpy as np
from jax import lax
from jax.experimental import pallas as pl
from jax.experimental.pallas import tpu as pltpu
from jax.sharding import PartitionSpec as P

AXES = ("row", "col")
SIDE = 4
LANES = 128

SLOTS = (
    (0, 0, 0),
    (3, 0, 0), (0, 1, 0), (0, 3, 0),
    (1, 1, 0), (3, 0, 1), (0, 3, 3),
    (3, 3, 3), (3, 1, 1), (3, 0, 2),
    (2, 3, 3), (1, 2, 0), (3, 1, 2),
)
PARENT = (None, 0, 0, 0, 2, 1, 3, 6, 5, 5, 7, 4, 8)
ROUNDS = ((0,), (1, 2, 3), (4, 6, 5), (7, 8, 9), (10, 11, 12))
OWN = (
    (0, 0, True), (9, 0, False), (3, 1, False), (4, 1, False), (6, 1, False), (7, 1, False), (9, 1, True),
    (3, 2, True), (4, 2, False), (6, 2, False), (7, 2, False), (9, 2, False), (9, 3, False), (0, 4, False),
    (5, 4, False), (9, 4, False), (0, 5, False), (9, 5, False), (8, 6, False), (10, 6, True), (11, 6, False),
    (3, 7, False), (4, 7, False), (5, 7, False), (8, 7, True), (3, 8, False), (4, 8, False), (5, 8, False),
    (8, 9, False), (10, 9, False), (11, 9, True), (0, 10, False), (1, 10, False), (0, 11, False), (1, 11, True),
    (4, 12, True),
)
CROSS = (
    (0, 0, 1), (4, 0, 0), (4, 0, 1), (6, 0, 0), (2, 1, 0), (2, 1, 1), (8, 1, 0), (9, 1, 0), (9, 1, 1),
    (2, 2, 0), (8, 2, 0), (8, 2, 1), (4, 3, 1), (6, 3, 0), (6, 3, 1), (7, 3, 0), (7, 3, 1), (1, 4, 0),
    (1, 4, 1), (2, 4, 1), (3, 4, 1), (6, 4, 0), (6, 4, 1), (8, 4, 0), (8, 4, 1), (1, 5, 0), (1, 5, 1),
    (2, 5, 0), (2, 5, 1), (3, 5, 1), (6, 5, 0), (6, 5, 1), (8, 5, 0), (8, 5, 1), (2, 6, 0), (2, 6, 1),
    (6, 6, 0), (7, 6, 1), (0, 7, 1), (8, 7, 1), (0, 8, 1), (8, 8, 1), (7, 9, 0), (7, 9, 1), (0, 10, 0),
    (1, 10, 1), (2, 10, 0), (2, 10, 1), (3, 10, 0), (3, 10, 1), (7, 10, 0), (8, 10, 0), (0, 11, 0), (0, 11, 1),
    (1, 11, 0), (1, 11, 1), (2, 11, 0), (2, 11, 1), (3, 11, 0), (3, 11, 1), (8, 11, 0), (8, 11, 1), (2, 12, 0),
    (2, 12, 1),
)
N_SLOTS = len(SLOTS)
PAIRS = ((0, 3), (1, 2), (4, 5), (6, 9), (7, 8), (10, 11), (12,))
OTHERS = tuple(sorted({j for j, _, _ in CROSS}))


def device_at(x, y, z, core):
    x, y, z, core = x % SIDE, y % SIDE, z % SIDE, core % 2
    return (x * 2 + y // 2) * 16 + z * 4 + (y % 2) * 2 + core


def places():
    for x in range(SIDE):
        for y in range(SIDE):
            for z in range(SIDE):
                for core in range(2):
                    yield x, y, z, core


def on_core(offset, core):
    x, y, z = offset
    return (-x, -z, -y) if core else offset


def minus(a, b):
    return tuple((i - j) % SIDE for i, j in zip(a, b))


def shift(value, offset):
    pairs = []
    for x, y, z, core in places():
        a, b, c = on_core(offset, core)
        pairs.append((device_at(x + a, y + b, z + c, core), device_at(x, y, z, core)))
    return lax.ppermute(value, AXES, pairs)


def swap(value):
    pairs = [(device_at(x, y, z, 1 - c), device_at(x, y, z, c)) for x, y, z, c in places()]
    return lax.ppermute(value, AXES, pairs)


def held_blocks():
    table = np.zeros((2 * SIDE**3, 2 * N_SLOTS), np.int32)
    for x, y, z, core in places():
        for k, offset in enumerate(SLOTS):
            for other in range(2):
                fam = core ^ other
                a, b, c = on_core(offset, fam)
                at = device_at(x + a, y + b, z + c, fam)
                table[device_at(x, y, z, core), k + other * N_SLOTS] = at
    return table


def pair_weights():
    weights = np.zeros((2, 2, 2 * N_SLOTS, N_SLOTS), np.float32)
    for left, right, one in OWN:
        weights[:, 0, left, right] = 1
        weights[:, 1, left, right] = 0 if one else 1
    for left, right, core in CROSS:
        weights[core, :, N_SLOTS + left, right] = 1
    return weights


def work_list():
    came = {slot: n for n, slots in enumerate(ROUNDS) for slot in slots}
    met = {}
    for left, right, _ in OWN:
        met.setdefault((max(came[left], came[right]), right), set()).add(left)
    for left, right, _ in CROSS:
        met.setdefault((max(came[left], came[right]), right), set()).add(N_SLOTS + left)
    work = []
    for n in range(len(ROUNDS)):
        here = []
        for pair in PAIRS:
            lefts = set().union(*(met.get((n, r), set()) for r in pair))
            rights = tuple(r for r in pair if came[r] <= n)
            if lefts:
                counted = {b: [r for r in rights if b in met.get((n, r), ())] for b in lefts}
                here.append((rights, sorted(lefts), counted))
        work.append(here)
    return work


def add_pairs(work, blocks, sums, weights, feats, homes=None):
    used = sorted({b for rights, lefts, _ in work for b in (*rights, *lefts)})
    n_tiles = sum(len(rights) * len(lefts) for rights, lefts, _ in work)
    scale = 1.0 / feats**0.5

    def body(w_ref, in_ref, *refs):
        out = refs[-1]
        if homes is not None:
            home_ref, refs = refs[0], refs[1:]
        ref = dict(zip(used, refs))
        out[...] = in_ref[...]
        eye = lax.broadcasted_iota(jnp.int32, (LANES, LANES), 0) == lax.broadcasted_iota(
            jnp.int32, (LANES, LANES), 1
        )

        def coeff(slot):
            return ref[slot][:, feats:].astype(jnp.float32)

        def along(wide):
            return jnp.sum(jnp.where(eye, wide, 0.0), axis=0, keepdims=True)

        def down(wide):
            return jnp.sum(jnp.where(eye, wide, 0.0), axis=1, keepdims=True)

        for rights, lefts, counted in work:
            right = [ref[r][:, :feats] for r in rights]
            right = right[0] if len(right) == 1 else jnp.concatenate(right, axis=0)
            right_coeff = [coeff(r)[0:1, :] for r in rights]
            for at in range(0, len(lefts), 2):
                some = lefts[at : at + 2]
                left = [ref[b][:, :feats] for b in some]
                left = left[0] if len(left) == 1 else jnp.concatenate(left, axis=0)
                inner = lax.dot_general(
                    left, right, (((1,), (1,)), ((), ())), preferred_element_type=jnp.float32
                )
                bent = jnp.tanh(inner * scale)
                for h, b in enumerate(some):
                    left_coeff = down(coeff(b))
                    back = jnp.zeros((LANES, LANES), jnp.float32)
                    for k, r in enumerate(rights):
                        if r not in counted[b]:
                            continue
                        part = bent[h * LANES : (h + 1) * LANES, k * LANES : (k + 1) * LANES]
                        got = jnp.sum(part * left_coeff, axis=0, keepdims=True)
                        out[r : r + 1, :] += w_ref[0, b, r] * got
                        back = back + part * (w_ref[1, b, r] * right_coeff[k])
                    wide = jnp.broadcast_to(jnp.sum(back, axis=1, keepdims=True), (LANES, LANES))
                    out[b : b + 1, :] += along(wide)

        if homes is not None:
            laid = refs[-2]
            laid[...] = jnp.zeros_like(laid)
            for k in range(2 * N_SLOTS):
                laid[pl.ds(home_ref[k], 1), :] = out[k : k + 1, :]

    smem = pl.BlockSpec(memory_space=pltpu.SMEM)
    vmem = pl.BlockSpec(memory_space=pltpu.VMEM)
    last = homes is not None
    kept = jax.ShapeDtypeStruct(sums.shape, jnp.float32)
    spread = jax.ShapeDtypeStruct((2 * SIDE**3, LANES), jnp.float32)
    return pl.pallas_call(
        body,
        out_shape=spread if last else kept,
        in_specs=[smem, vmem] + ([smem] if last else []) + [vmem] * len(used),
        out_specs=vmem,
        scratch_shapes=[pltpu.VMEM(sums.shape, jnp.float32)] if last else [],
        compiler_params=pltpu.CompilerParams(vmem_limit_bytes=24 * 2**20),
        cost_estimate=pl.CostEstimate(
            flops=2 * n_tiles * LANES * LANES * feats,
            bytes_accessed=2 * len(used) * LANES * feats,
            transcendentals=n_tiles * LANES * LANES,
        ),
    )(weights, sums, *([homes] if last else []), *[blocks[b] for b in used])


def on_device(grads, coeffs, band, steps):
    rows_here, feats = grads.shape
    width = band[0]
    me = lax.axis_index(AXES)
    held = lax.dynamic_index_in_dim(jnp.asarray(held_blocks()), me, 0, keepdims=False)
    hit = held[:, None] == jnp.arange(steps.shape[0], dtype=jnp.int32)[None, :]
    held_steps = jnp.sum(jnp.where(hit, steps[None, :], 0), axis=1)
    near = jnp.abs(held_steps[:, None] - held_steps[None, :N_SLOTS]) <= width
    table = pair_weights()
    weights = jnp.where(me % 2 == 0, table[0], table[1])
    weights = jnp.where(near[None], weights, 0.0)
    count = rows_here * jnp.sum((jnp.abs(steps - held_steps[0]) <= width).astype(jnp.int32))

    divisor = jnp.sqrt(count.astype(jnp.float32))
    weights, divisor = lax.optimization_barrier((weights, divisor))
    wide = jnp.broadcast_to(coeffs[None, :], (LANES, rows_here))
    blocks = {0: jnp.concatenate([grads, wide], axis=1)}
    sums = jnp.zeros((2 * N_SLOTS, LANES), jnp.float32)
    work = work_list()

    def held_back(value, until):
        for u in until:
            value, _ = lax.optimization_barrier((value, u))
        return value

    if 0 in OTHERS:
        blocks[N_SLOTS] = swap(blocks[0])
    for n in range(1, len(ROUNDS)):
        until = [blocks[slot] for slot in ROUNDS[n - 1]] if n > 1 else []
        for at, slot in enumerate(ROUNDS[n]):
            parent = PARENT[slot]
            blocks[slot] = shift(
                held_back(blocks[parent], until[at : at + 1]), minus(SLOTS[slot], SLOTS[parent])
            )
        if n == 3:
            sums = add_pairs(work[0] + work[1], blocks, sums, weights, feats)
            until = until[:2] + [sums]
        if n == 4:
            sums = jnp.where(width < 0, 0.0, held_back(sums, until))
            until = until + [sums]
        for slot in ROUNDS[n - 1] if n > 1 else ():
            if slot in OTHERS:
                blocks[N_SLOTS + slot] = swap(held_back(blocks[slot], until))
    sums = add_pairs(work[2] + work[3], blocks, sums, weights, feats)
    parts = add_pairs(work[4], blocks, sums, weights, feats, held)
    total = jnp.sum(lax.all_to_all(parts, AXES, 0, 0, tiled=True), axis=0)
    return total.reshape(-1) / divisor


def solution(mesh):
    in_specs = (P(AXES, None), P(AXES), P(), P())
    out_specs = P(AXES)
    return jax.shard_map(
        on_device, mesh=mesh, in_specs=in_specs, out_specs=out_specs, check_vma=False
    )
```
